256 devices in a mesh: fsdp: 16 (over x, y), rep: 16 (over z, core).
Axes of the slice: x: 4, y: 4, z: 8, core: 2. Of those that a mesh axis runs over, the one named last changes fastest.
Arguments:
- momentum: float32 [28672, 8192], P('fsdp', 'rep'), may hold values from -6 to 6
- gradient: bfloat16 [28672, 8192], P('fsdp', 'rep'), may hold values from -6 to 6
- right_factor: float32 [8192, 256], P('rep'), may hold values from -6 to 6
Outputs:
- new_momentum: float32 [28672, 8192], P('fsdp', 'rep')
- new_factor: float32 [8192, 256], P('rep')
- update: bfloat16 [28672, 8192], P('fsdp', 'rep')
The draws below stay inside these ranges and needn't reach their ends.
All inputs are finite; a program needn't handle non-finite values.
Results may differ from the reference program's by a relative error of at most 0.0014.
Values sent between devices are 32-bit elements; how exact they have to be, the bound alone decides.
A program may use at most 64 MiB of HBM per device.

```python
import math
import jax
import jax.numpy as jnp
from jax import lax

D = 8192
FF = 28672
R = 256


def level_of(stream_key, shape, shards, least, largest):
    gain = 1.0
    for axis_at, blocks in shards:
        steps = jax.random.uniform(jax.random.fold_in(jax.random.fold_in(stream_key, 6), axis_at), (blocks,), jnp.float32, least / len(shards), largest / len(shards))
        gain = gain * jnp.repeat(jnp.exp(steps), shape[axis_at] // blocks).reshape((-1,) + (1,) * (len(shape) - 1 - axis_at))
    return gain


def centred(own_key, dims, deviation, bound, split=(), held_as=jnp.bfloat16):
    loudness = level_of(own_key, dims, split, -0.22, 0.18) if split else 1.0
    array = jax.random.normal(own_key, dims, jnp.float32) * deviation * loudness
    return jnp.minimum(jnp.maximum(array, -bound), bound).astype(held_as)


def setup_inputs(seed: int = 0) -> dict:
    key_of = jax.random.split(jax.random.key(seed), 4)
    return {
        "momentum": centred(key_of[0], (FF, D), 1.0, 6.0, ((0, 16), (1, 16)), jnp.float32),
        "gradient": centred(key_of[1], (FF, D), 1.0, 6.0, ((0, 16), (1, 16))),
        "right_factor": centred(key_of[2], (D, R), 1.0, 6.0, ((0, 16),), jnp.float32),
    }


keep_share = 0.05
step_size = 0.5
norm_eps = 1e-06

def reference(momentum, gradient, right_factor):
    precise = lax.Precision.HIGHEST
    combined = momentum + gradient.astype(jnp.float32)
    raw_factor = jnp.dot(combined, right_factor, precision=precise)
    gram_matrix = jnp.dot(raw_factor.T, raw_factor, precision=precise)
    triangle = jnp.linalg.cholesky(gram_matrix)
    left_factor = lax.linalg.triangular_solve(triangle, raw_factor, left_side=False, lower=True, transpose_a=True)
    cross_term = jnp.dot(combined.T, left_factor, precision=precise)
    new_momentum = combined - keep_share * jnp.dot(left_factor, cross_term.T, precision=precise)
    column_sums = lax.optimization_barrier(jnp.sum(cross_term * cross_term, axis=0))
    new_factor = cross_term / jnp.sqrt(column_sums / D + norm_eps)
    update = (-step_size * math.sqrt(FF / R) * jnp.dot(left_factor, new_factor.T, precision=precise)).astype(jnp.bfloat16)
    return (new_momentum, new_factor, update)
```

```python
import functools
import math

import jax
import jax.numpy as jnp
from jax import lax
from jax.experimental import pallas as pl
from jax.experimental.pallas import tpu as pltpu
from jax.sharding import PartitionSpec as P

D = 8192
FF = 28672
R = 256

keep_share = 0.05
step_size = 0.5
norm_eps = 1e-06

F32 = jnp.float32
BF16 = jnp.bfloat16
MESH = pl.DeviceIdType.MESH
HIGHEST = lax.Precision.HIGHEST

ROWS = 1792
COLS = 512
NZ = 8
NF = 16
NR = 16
PAIR = ROWS // NZ
OWN = PAIR // 2
SUB = OWN // 2
NB = 32


def split(x):
    hi = x.astype(BF16)
    return hi, (x - hi.astype(F32)).astype(BF16)


def dot(a, b, dims=((1,), (0,)), precision=None):
    return lax.dot_general(a, b, (dims, ((), ())), precision=precision, preferred_element_type=F32)


def dot3(a, b, dims=((1,), (0,))):
    return dot(a[0], b[0], dims) + (dot(a[1], b[0], dims) + dot(a[0], b[1], dims))


def factor_panel(rows, base):
    lane = lax.broadcasted_iota(jnp.int32, (8, 128), 1)
    sub = lax.broadcasted_iota(jnp.int32, (8, 128), 0)
    n = len(rows)
    for j in range(n):
        l0 = base + 8 * j
        half, at = l0 // 128, l0 % 128
        cols = [
            [jnp.broadcast_to(rows[i][half][:, at + c : at + c + 1], (8, 128)) for c in range(8)]
            for i in range(j, n)
        ]
        s = [
            [jnp.broadcast_to(cols[0][c][r : r + 1, :], (8, 128)) if r >= c else None for c in range(8)]
            for r in range(8)
        ]
        inv, low, solved = [None] * 8, [[None] * 8 for _ in range(8)], []
        own = (lane >= at) & (lane < at + 8)
        v = list(rows[j])
        v[half] = jnp.where(own, jnp.where(lane - at == sub, 1.0, 0.0), v[half])
        for p in range(8):
            inv[p] = lax.rsqrt(s[p][p])
            for r in range(p + 1, 8):
                low[r][p] = s[r][p] * inv[p]
            for r in range(p + 1, 8):
                for c in range(p + 1, r + 1):
                    s[r][c] = s[r][c] - low[r][p] * low[c][p]
            x = [jnp.broadcast_to(v[h][p : p + 1, :], (8, 128)) for h in range(2)]
            for q in range(p):
                x = [x[h] - low[p][q] * solved[q][h] for h in range(2)]
            solved.append([x[h] * inv[p] for h in range(2)])
        for i in range(j + 1, n):
            w, coef = list(rows[i]), []
            w[half] = jnp.where(own, 0.0, w[half])
            for p in range(8):
                t = cols[i - j][p]
                for q in range(p):
                    t = t - coef[q] * low[p][q]
                coef.append(t * inv[p])
            for p in range(8):
                w = [w[h] - coef[p] * solved[p][h] for h in range(2)]
            rows[i] = w
        out = []
        for h in range(2):
            a = solved[0][h]
            for p in range(1, 8):
                a = jnp.where(sub == p, solved[p][h], a)
            out.append(a)
        rows[j] = out
    return rows


def chol_step(M, k):
    r0, end = NB * k, NB * (k + 1)
    rows = [
        [M[r0 + 8 * j : r0 + 8 * j + 8, 128 * h : 128 * h + 128] for h in range(2)] for j in range(NB // 8)
    ]
    rows = factor_panel(rows, r0)
    for j in range(NB // 8):
        for h in range(2):
            M[r0 + 8 * j : r0 + 8 * j + 8, 128 * h : 128 * h + 128] = rows[j][h]
    if end == R:
        return
    panel = M[r0:end, :]
    row = lax.broadcasted_iota(jnp.int32, (NB, R), 0) + r0
    col = lax.broadcasted_iota(jnp.int32, (NB, R), 1)
    right = jnp.where((col < end) & (col > row), 0.0, panel)
    lo = (end // 128) * 128
    left = jnp.swapaxes(panel[:, lo:], 0, 1)[end - lo :, :]
    old = M[end:, :]
    at = lax.broadcasted_iota(jnp.int32, old.shape, 1)
    old = jnp.where((at >= r0) & (at < end), 0.0, old)
    M[end : end + NB, :] = old[:NB] - dot(left[:NB], right, precision=HIGHEST)
    if end + NB < R:
        M[end + NB :, :] = old[NB:] - dot(left[NB:], right, precision=HIGHEST)


def gather_kernel(
    mom, grad, q_ref, u_out, wt_out, inv_out,
    momb, gradb, chi, clo, part, sib, rsr, pfull, gp, g1, g2, gf, M, yp, yr, yf, y8, g16, ubuf, cs, csr,
    ld_sem, sib_s, sib_r, rs_s, rs_r, ag_s, ag_r, sb_s, sb_r, g_s, g_r, y_s, y_r, n_s, n_r, u_s,
):
    f, r = lax.axis_index("fsdp"), lax.axis_index("rep")
    z, c = r // 2, r % 2
    sibling = (f, z * 2 + 1 - c)
    up, down = (f, ((z + 1) % NZ) * 2 + c), (f, ((z + NZ - 1) % NZ) * 2 + c)
    ring = (up, down)
    mine = pl.multiple_of(c * OWN, 8)
    other = pl.multiple_of((1 - c) * OWN, 8)

    def remote(src, dst, ss, rs, to):
        return pltpu.make_async_remote_copy(src, dst, ss, rs, device_id=to, device_id_type=MESH)

    barrier = pltpu.get_barrier_semaphore()

    @pl.loop(1, 16)
    def _(k):
        pl.semaphore_signal(barrier, 1, device_id=(f, (r + k) % NR), device_id_type=MESH)
        pl.semaphore_signal(barrier, 1, device_id=((f + k) % NF, r), device_id_type=MESH)

    order = (4, 3, 5, 2, 6, 1, 7, 0)
    loads = {}
    for o in order:
        zd = (z + o) % NZ
        at = pl.ds(pl.multiple_of(zd * PAIR, PAIR), PAIR)
        loads[o] = (
            pltpu.make_async_copy(mom.at[at], momb.at[o], ld_sem.at[0, o]),
            pltpu.make_async_copy(grad.at[at], gradb.at[o], ld_sem.at[1, o]),
        )
        for copy in loads[o]:
            copy.start()
    q = split(q_ref[...])
    sends = []

    def go(copy):
        copy.start()
        sends.append(copy)
        return copy

    sib_copy = {}
    pl.semaphore_wait(barrier, 30)

    def compute(o):
        for copy in loads[o]:
            copy.wait()
        zd = (z + o) % NZ
        both = split(momb[o] + gradb[o].astype(F32))
        chi[zd] = both[0]
        clo[zd] = both[1]
        part[o] = dot3(both, q)
        sib_copy[o] = go(
            remote(part.at[o, pl.ds(other, OWN)], sib.at[o], sib_s.at[o], sib_r.at[o], sibling)
        )

    def add_sibling(o):
        sib_copy[o].wait_recv()
        part[o, pl.ds(mine, OWN)] = part[o, pl.ds(mine, OWN)] + sib[o]

    def sub_at(s):
        return pl.ds(pl.multiple_of(c * OWN + s * SUB, 8), SUB)

    def offset(way, level):
        return level if way == 0 else (NZ - level) % NZ

    rs_copy = {}

    def rs_send(way, level, s):
        rs_copy[way, level, s] = go(
            remote(
                part.at[offset(way, level), sub_at(s)],
                rsr.at[way, level - 1, s],
                rs_s.at[way, level - 1, s],
                rs_r.at[way, level - 1, s],
                ring[way],
            )
        )

    def rs_add(way, level, s):
        rs_copy[way, level + 1, s].wait_recv()
        o = offset(way, level)
        part[o, sub_at(s)] = part[o, sub_at(s)] + rsr[way, level, s]

    compute(4)
    compute(3)
    add_sibling(4)
    rs_send(0, 4, 0)
    rs_send(1, 4, 1)
    compute(5)
    add_sibling(3)
    rs_send(0, 3, 1)
    compute(2)
    add_sibling(5)
    rs_send(1, 3, 0)
    compute(6)
    add_sibling(2)
    compute(1)
    add_sibling(6)
    for way in range(2):
        rs_add(way, 3, way)
        rs_send(way, 3, way)
    compute(7)
    add_sibling(1)
    compute(0)
    add_sibling(7)
    add_sibling(0)
    for level in (2, 1):
        for s_of in (lambda way: 1 - way, lambda way: way):
            for way in range(2):
                rs_add(way, level, s_of(way))
                rs_send(way, level, s_of(way))
    for s in range(2):
        for way in range(2):
            rs_add(way, 0, s if way == 1 else 1 - s)

    own_rows = part[0, pl.ds(mine, OWN), :]
    for h in range(2):
        pfull[h, z, pl.ds(mine, OWN), :] = own_rows[:, 128 * h : 128 * h + 128]
    ag_copy, sb_copy = {}, {}

    def ag_send(way, level, h):
        zs = (z + (NZ - (level - 1) if way == 0 else level - 1)) % NZ
        ref = pfull.at[h, zs, pl.ds(mine, OWN) if level < 4 else sub_at(way)]
        ag_copy[way, level, h] = go(
            remote(ref, ref, ag_s.at[way, level - 1, h], ag_r.at[way, level - 1, h], ring[way])
        )

    def sb_send(way, level, h):
        zs = (z + (NZ - level if way == 0 else level)) % NZ
        ref = pfull.at[h, zs, pl.ds(mine, OWN)]
        sb_copy[way, level, h] = go(remote(ref, ref, sb_s.at[way, level, h], sb_r.at[way, level, h], sibling))

    for h in range(2):
        for way in range(2):
            ag_send(way, 1, h)
    for h in range(2):
        sb_send(0, 0, h)

    def to_all(src_of, dst, send, recv, along):
        me = r if along == "rep" else f

        @pl.loop(1, 16)
        def _(k):
            peer = (me + k) % 16
            to = (f, peer) if along == "rep" else (peer, r)
            remote(src_of(peer), dst.at[me], send, recv, to).start()

    def all_arrived(dst, send, recv):
        span = dst.at[pl.ds(0, 15)]
        pltpu.make_async_copy(span, span, recv).wait()

    def all_sent(dst, send):
        span = dst.at[pl.ds(0, 15)]
        pltpu.make_async_copy(span, span, send).wait()

    def total(ref):
        t = ref[0]
        for k in range(1, 16):
            t = t + ref[k]
        return t

    gp[...] = dot(own_rows, own_rows, ((0,), (0,)), HIGHEST).reshape(16, 16, R)
    to_all(lambda peer: gp.at[peer], g1, g_s.at[0], g_r.at[0], "rep")
    g1[pl.ds(r, 1)] = gp[pl.ds(r, 1)]

    def ag_forward(level):
        for h in range(2):
            for way in range(2):
                ag_copy[way, level, h].wait_recv()
                if level < 4:
                    ag_send(way, level + 1, h)
                    sb_send(way, level, h)
            if level == 4:
                sb_send(0, 4, h)

    def y_add(zs, h, first=False):
        p = split(jnp.swapaxes(pfull[h, zs], 0, 1))
        y = dot3(p, (chi[zs], clo[zs]))
        yp[h] = y if first else yp[h] + y

    def y_level(level, h):
        for way in range(2 if 0 < level < 4 else 1):
            sb_copy[way, level, h].wait_recv()
            y_add((z + (NZ - level if way == 0 else level)) % NZ, h, level == 0)

    ag_forward(1)
    all_arrived(g1, g_s.at[0], g_r.at[0])
    g16[0] = total(g1)
    to_all(lambda peer: g16.at[0], g2, g_s.at[1], g_r.at[1], "fsdp")
    g2[pl.ds(f, 1)] = g16[pl.ds(0, 1)]
    for h in range(2):
        y_level(0, h)
    ag_forward(2)
    for h in range(2):
        y_level(1, h)
    all_arrived(g2, g_s.at[1], g_r.at[1])
    g16[1] = total(g2)
    to_all(lambda peer: g16.at[1], gf, g_s.at[2], g_r.at[2], "rep")
    gf[pl.ds(r, 1)] = g16[pl.ds(1, 1)]
    ag_forward(3)
    for h in range(2):
        y_level(2, h)
    ag_forward(4)
    for h in range(2):
        y_level(3, h)
        y_level(4, h)
        to_all(lambda peer: yp.at[h, pl.ds(pl.multiple_of(peer * 8, 8), 8)], yr.at[h], y_s.at[h], y_r.at[h], "fsdp")
        yr[h, pl.ds(f, 1)] = yp[h, pl.ds(pl.multiple_of(f * 8, 8), 8)].reshape(1, 8, COLS)
    all_arrived(gf, g_s.at[2], g_r.at[2])
    M[...] = gf[...].reshape(R, R)
    for k in range(4):
        chol_step(M, k)
    for h in range(2):
        all_arrived(yr.at[h], y_s.at[h], y_r.at[h])
        y8[h] = total(yr.at[h])
        to_all(lambda peer: y8.at[h], yf.at[h], y_s.at[2 + h], y_r.at[2 + h], "fsdp")
        yf[h, pl.ds(f, 1)] = y8[pl.ds(h, 1)]
    for k in range(4, R // NB):
        chol_step(M, k)
    row = lax.broadcasted_iota(jnp.int32, (R, R), 0)
    col = lax.broadcasted_iota(jnp.int32, (R, R), 1)
    linv = split(jnp.where(col <= row, M[...], 0.0))
    for h in range(2):
        all_arrived(yf.at[h], y_s.at[2 + h], y_r.at[2 + h])
    wt = dot3(linv, split(yf[...].reshape(R, COLS)))
    wt_out[...] = wt
    cs[...] = dot(jnp.ones((8, COLS), F32), wt * wt, ((1,), (1,)), HIGHEST)
    to_all(lambda peer: cs, csr, n_s, n_r, "rep")
    csr[pl.ds(r, 1)] = cs[...].reshape(1, 8, R)

    M[...] = jnp.where(col <= row, M[...], 0.0)

    @pl.loop(0, NZ)
    def _(zs):
        t = jnp.concatenate([pfull[0, zs], pfull[1, zs]], axis=1)
        ubuf[zs] = dot3(split(t), split(M[...]), ((1,), (1,)))
        pltpu.make_async_copy(ubuf.at[zs], u_out.at[zs], u_s).start()

    all_arrived(csr, n_s, n_r)
    inv_out[...] = 1.0 / jnp.sqrt(total(csr) / D + norm_eps)
    pltpu.make_async_copy(ubuf, u_out, u_s).wait()
    for copy in sends:
        copy.wait_send()
    all_sent(g1, g_s.at[0])
    all_sent(g2, g_s.at[1])
    all_sent(gf, g_s.at[2])
    for h in range(2):
        all_sent(yr.at[h], y_s.at[h])
        all_sent(yf.at[h], y_s.at[2 + h])
    all_sent(csr, n_s)


def gather(mom, grad, q):
    dma = pltpu.SemaphoreType.DMA
    vm = pltpu.VMEM
    scratch = [
        vm((NZ, PAIR, COLS), F32), vm((NZ, PAIR, COLS), BF16), vm((NZ, PAIR, COLS), BF16), vm((NZ, PAIR, COLS), BF16),
        vm((NZ, PAIR, R), F32), vm((NZ, OWN, R), F32), vm((2, 4, 2, SUB, R), F32), vm((2, NZ, PAIR, 128), F32),
        vm((16, 16, R), F32), vm((16, 16, R), F32), vm((16, 16, R), F32), vm((16, 16, R), F32), vm((R, R), F32),
        vm((2, 128, COLS), F32), vm((2, 16, 8, COLS), F32), vm((2, 16, 8, COLS), F32), vm((2, 8, COLS), F32),
        vm((2, 16, R), F32), vm((NZ, PAIR, R), F32), vm((8, R), F32), vm((16, 8, R), F32),
        dma((2, NZ)), dma((NZ,)), dma((NZ,)), dma((2, 4, 2)), dma((2, 4, 2)), dma((2, 4, 2)), dma((2, 4, 2)),
        dma((2, 5, 2)), dma((2, 5, 2)), dma((3,)), dma((3,)), dma((4,)), dma((4,)), dma, dma, dma,
    ]
    whole, hbm = pl.BlockSpec(memory_space=pltpu.VMEM), pl.BlockSpec(memory_space=pl.ANY)
    return pl.pallas_call(
        gather_kernel,
        name="gather",
        out_shape=(
            jax.ShapeDtypeStruct((NZ, PAIR, R), F32),
            jax.ShapeDtypeStruct((R, COLS), F32),
            jax.ShapeDtypeStruct((8, R), F32),
        ),
        in_specs=[hbm, hbm, whole],
        out_specs=(hbm, whole, whole),
        scratch_shapes=scratch,
        compiler_params=pltpu.CompilerParams(
            collective_id=0, has_side_effects=True, vmem_limit_bytes=48 << 20
        ),
    )(mom, grad, q)


def result_kernel(mom, grad, u_ref, wt_ref, inv_ref, new_mom, new_factor, update, wh, wl):
    inv = inv_ref[0:1, :]

    @pl.when(pl.program_id(0) == 0)
    def _():
        wh[...], wl[...] = split(wt_ref[...])
        new_factor[...] = jnp.swapaxes(wt_ref[...], 0, 1) * inv

    u = u_ref[...]
    combined = mom[...] + grad[...].astype(F32)
    new_mom[...] = combined - keep_share * dot(u.astype(BF16), wh[...])
    scaled = split(u * (inv * (-step_size * math.sqrt(FF / R))))
    update[...] = dot3(scaled, (wh[...], wl[...])).astype(BF16)


def results(mom, grad, u, wt, inv):
    rows = 256

    def tile(cols):
        return pl.BlockSpec((rows, cols), lambda i: (i, 0))

    def fixed(shape):
        return pl.BlockSpec(shape, lambda i: (0, 0))

    return pl.pallas_call(
        result_kernel,
        name="results",
        grid=(ROWS // rows,),
        out_shape=(
            jax.ShapeDtypeStruct((ROWS, COLS), F32),
            jax.ShapeDtypeStruct((COLS, R), F32),
            jax.ShapeDtypeStruct((ROWS, COLS), BF16),
        ),
        in_specs=[tile(COLS), tile(COLS), tile(R), fixed((R, COLS)), fixed((8, R))],
        out_specs=(tile(COLS), fixed((COLS, R)), tile(COLS)),
        scratch_shapes=[pltpu.VMEM((R, COLS), BF16), pltpu.VMEM((R, COLS), BF16)],
        compiler_params=pltpu.CompilerParams(vmem_limit_bytes=32 << 20),
    )(mom, grad, u, wt, inv)


def local(momentum, gradient, right_factor):
    u, wt, inv = gather(momentum, gradient, right_factor)
    return results(momentum, gradient, u.reshape(ROWS, R), wt, inv)


def solution(mesh):
    in_specs = (P("fsdp", "rep"), P("fsdp", "rep"), P("rep", None))
    out_specs = (P("fsdp", "rep"), P("rep", None), P("fsdp", "rep"))
    return jax.shard_map(local, mesh=mesh, in_specs=in_specs, out_specs=out_specs, check_vma=False)
```

```python
import functools
import math

import jax
import jax.numpy as jnp
from jax import lax
from jax.experimental import pallas as pl
from jax.experimental.pallas import tpu as pltpu
from jax.sharding import PartitionSpec as P

D = 8192
FF = 28672
R = 256

keep_share = 0.05
step_size = 0.5
norm_eps = 1e-06

F32 = jnp.float32
BF16 = jnp.bfloat16
MESH = pl.DeviceIdType.MESH
HIGHEST = lax.Precision.HIGHEST

ROWS = 1792
COLS = 512
NZ = 8
NF = 16
NR = 16
PAIR = ROWS // NZ
OWN = PAIR // 2
SUB = OWN // 2
NB = 32
TILE = 128


def split(x):
    hi = x.astype(BF16)
    return hi, (x - hi.astype(F32)).astype(BF16)


def dot(a, b, dims=((1,), (0,)), precision=None):
    return lax.dot_general(a, b, (dims, ((), ())), precision=precision, preferred_element_type=F32)


def dot3(a, b, dims=((1,), (0,))):
    return dot(a[0], b[0], dims) + (dot(a[1], b[0], dims) + dot(a[0], b[1], dims))


def factor_panel(rows, base):
    lane = lax.broadcasted_iota(jnp.int32, (8, 128), 1)
    sub = lax.broadcasted_iota(jnp.int32, (8, 128), 0)
    n = len(rows)
    for j in range(n):
        l0 = base + 8 * j
        half, at = l0 // 128, l0 % 128
        cols = [
            [jnp.broadcast_to(rows[i][half][:, at + c : at + c + 1], (8, 128)) for c in range(8)]
            for i in range(j, n)
        ]
        s = [
            [jnp.broadcast_to(cols[0][c][r : r + 1, :], (8, 128)) if r >= c else None for c in range(8)]
            for r in range(8)
        ]
        inv, low, solved = [None] * 8, [[None] * 8 for _ in range(8)], []
        own = (lane >= at) & (lane < at + 8)
        v = list(rows[j])
        v[half] = jnp.where(own, jnp.where(lane - at == sub, 1.0, 0.0), v[half])
        for p in range(8):
            inv[p] = lax.rsqrt(s[p][p])
            for r in range(p + 1, 8):
                low[r][p] = s[r][p] * inv[p]
            for r in range(p + 1, 8):
                for c in range(p + 1, r + 1):
                    s[r][c] = s[r][c] - low[r][p] * low[c][p]
            x = [jnp.broadcast_to(v[h][p : p + 1, :], (8, 128)) for h in range(2)]
            for q in range(p):
                x = [x[h] - low[p][q] * solved[q][h] for h in range(2)]
            solved.append([x[h] * inv[p] for h in range(2)])
        for i in range(j + 1, n):
            w, coef = list(rows[i]), []
            w[half] = jnp.where(own, 0.0, w[half])
            for p in range(8):
                t = cols[i - j][p]
                for q in range(p):
                    t = t - coef[q] * low[p][q]
                coef.append(t * inv[p])
            for p in range(8):
                w = [w[h] - coef[p] * solved[p][h] for h in range(2)]
            rows[i] = w
        out = []
        for h in range(2):
            a = solved[0][h]
            for p in range(1, 8):
                a = jnp.where(sub == p, solved[p][h], a)
            out.append(a)
        rows[j] = out
    return rows


def chol_step(M, k):
    r0, end = NB * k, NB * (k + 1)
    rows = [
        [M[r0 + 8 * j : r0 + 8 * j + 8, 128 * h : 128 * h + 128] for h in range(2)] for j in range(NB // 8)
    ]
    rows = factor_panel(rows, r0)
    for j in range(NB // 8):
        for h in range(2):
            M[r0 + 8 * j : r0 + 8 * j + 8, 128 * h : 128 * h + 128] = rows[j][h]
    if end == R:
        return
    panel = M[r0:end, :]
    row = lax.broadcasted_iota(jnp.int32, (NB, R), 0) + r0
    col = lax.broadcasted_iota(jnp.int32, (NB, R), 1)
    right = jnp.where((col < end) & (col > row), 0.0, panel)
    lo = (end // 128) * 128
    left = jnp.swapaxes(panel[:, lo:], 0, 1)[end - lo :, :]
    old = M[end:, :]
    at = lax.broadcasted_iota(jnp.int32, old.shape, 1)
    old = jnp.where((at >= r0) & (at < end), 0.0, old)
    M[end : end + NB, :] = old[:NB] - dot(left[:NB], right, precision=HIGHEST)
    if end + NB < R:
        M[end + NB :, :] = old[NB:] - dot(left[NB:], right, precision=HIGHEST)


def gather_kernel(
    mom, grad, q_hbm, nm_out, u_out, wt_out, inv_out,
    momb, gradb, qb, chi, clo, part, sib, rsr, pfull, gp, g1, g2, gs, gf, M, yp, yr, yf, y8, g16, cs, csr,
    ld_sem, q_sem, sib_s, sib_r, rs_s, rs_r, ag_s, ag_r, sb_s, sb_r, g_s, g_r, y_s, y_r, n_s, n_r,
):
    f, r = lax.axis_index("fsdp"), lax.axis_index("rep")
    z, c = r // 2, r % 2
    sibling = (f, z * 2 + 1 - c)
    ring = ((f, ((z + 1) % NZ) * 2 + c), (f, ((z + NZ - 1) % NZ) * 2 + c))
    mine = pl.multiple_of(c * OWN, 8)
    other = pl.multiple_of((1 - c) * OWN, 8)
    HALVES, WAYS = range(2), range(2)

    def lanes(h):
        return pl.ds(128 * h, 128)

    def sub_at(s):
        return pl.ds(pl.multiple_of(c * OWN + s * SUB, 8), SUB)

    def remote(src, dst, ss, rs, to):
        return pltpu.make_async_remote_copy(src, dst, ss, rs, device_id=to, device_id_type=MESH)

    q_load = pltpu.make_async_copy(q_hbm, qb, q_sem)
    q_load.start()
    loads = {}
    for o in (4, 3, 5, 2, 6, 1, 7, 0):
        zd = (z + o) % NZ
        at = pl.ds(pl.multiple_of(zd * PAIR, PAIR), PAIR)
        loads[o] = (
            pltpu.make_async_copy(mom.at[at], momb.at[o], ld_sem.at[0, o]),
            pltpu.make_async_copy(grad.at[at], gradb.at[o], ld_sem.at[1, o]),
        )
        for copy in loads[o]:
            copy.start()

    barrier = pltpu.get_barrier_semaphore()

    @pl.loop(1, 16)
    def _(k):
        pl.semaphore_signal(barrier, 1, device_id=(f, (r + k) % NR), device_id_type=MESH)
        pl.semaphore_signal(barrier, 1, device_id=((f + k) % NF, r), device_id_type=MESH)

    q_load.wait()
    q = split(qb[...])
    sends = []

    def go(copy):
        copy.start()
        sends.append(copy)
        return copy

    sib_copy = {}

    def compute(o):
        for copy in loads[o]:
            copy.wait()
        zd = (z + o) % NZ
        combined = momb[o] + gradb[o].astype(F32)
        momb[o] = combined
        both = split(combined)
        chi[zd] = both[0]
        clo[zd] = both[1]
        part[o] = dot3(both, q)

    def to_sibling(o):
        sib_copy[o] = go(
            remote(part.at[o, pl.ds(other, OWN)], sib.at[o], sib_s.at[o], sib_r.at[o], sibling)
        )

    def add_sibling(o):
        sib_copy[o].wait_recv()
        part[o, pl.ds(mine, OWN)] = part[o, pl.ds(mine, OWN)] + sib[o]

    def offset(way, level):
        return level if way == 0 else (NZ - level) % NZ

    rs_copy = {}

    def rs_send(way, level, s, h):
        at = (way, level - 1, h, s)
        rs_copy[at] = go(
            remote(
                part.at[offset(way, level), sub_at(s), lanes(h)],
                rsr.at[at], rs_s.at[at], rs_r.at[at], ring[way],
            )
        )

    def rs_add(way, level, s, h):
        at = (way, level, h, s)
        rs_copy[at].wait_recv()
        o = offset(way, level)
        part[o, sub_at(s), lanes(h)] = part[o, sub_at(s), lanes(h)] + rsr[at]

    def rs_pass(level, late):
        for h in HALVES:
            for way in WAYS:
                s = way if late else 1 - way
                rs_add(way, level, s, h)
                rs_send(way, level, s, h)

    compute(4)
    compute(3)
    pl.semaphore_wait(barrier, 30)
    to_sibling(4)
    to_sibling(3)
    compute(5)
    to_sibling(5)
    add_sibling(4)
    for h in HALVES:
        for way in WAYS:
            rs_send(way, 4, way, h)
    add_sibling(3)
    for h in HALVES:
        rs_send(0, 3, 1, h)
    add_sibling(5)
    for h in HALVES:
        rs_send(1, 3, 0, h)
    compute(2)
    to_sibling(2)
    compute(6)
    to_sibling(6)
    compute(1)
    to_sibling(1)
    add_sibling(2)
    add_sibling(6)
    rs_pass(3, True)
    compute(7)
    to_sibling(7)
    rs_pass(2, False)
    compute(0)
    to_sibling(0)
    add_sibling(1)
    add_sibling(7)
    rs_pass(2, True)
    rs_pass(1, False)
    add_sibling(0)
    rs_pass(1, True)

    ag_copy, sb_copy = {}, {}

    def source(way, level):
        return (z + (NZ - level if way == 0 else level)) % NZ

    def ag_send(way, level, h, s):
        at = (way, level - 1, h, s)
        ref = pfull.at[h, source(way, level - 1), sub_at(s)]
        ag_copy[at] = go(remote(ref, ref, ag_s.at[at], ag_r.at[at], ring[way]))

    def sb_send(way, level, h):
        rows = sub_at(way) if level == 4 else pl.ds(mine, OWN)
        ref = pfull.at[h, source(way, level), rows]
        at = (way, level, h)
        sb_copy[at] = go(remote(ref, ref, sb_s.at[at], sb_r.at[at], sibling))

    for h in HALVES:
        for late in (False, True):
            for way in WAYS:
                rs_add(way, 0, way if late else 1 - way, h)
        pfull[h, z, pl.ds(mine, OWN), :] = part[0, pl.ds(mine, OWN), lanes(h)]
        for s in range(2):
            for way in WAYS:
                ag_send(way, 1, h, s)
        sb_send(0, 0, h)

    def to_all(src_of, dst, send, recv, along):
        me, n = {"rep": (r, NR), "fsdp": (f, NF), "z": (z, NZ)}[along]

        @pl.loop(1, n)
        def _(k):
            peer = (me + k) % n
            to = {"rep": (f, peer), "fsdp": (peer, r), "z": (f, peer * 2 + c)}[along]
            remote(src_of(peer), dst.at[me], send, recv, to).start()

    def span_wait(dst, sem):
        span = dst.at[pl.ds(0, dst.shape[0] - 1)]
        pltpu.make_async_copy(span, span, sem).wait()

    def total(ref):
        t = ref[0]
        for k in range(1, ref.shape[0]):
            t = t + ref[k]
        return t

    own_rows = part[0, pl.ds(mine, OWN), :]
    gp[...] = dot(own_rows, own_rows, ((0,), (0,)), HIGHEST).reshape(16, 16, R)
    to_all(lambda peer: gp.at[peer], g1, g_s.at[0], g_r.at[0], "fsdp")
    g1[pl.ds(f, 1)] = gp[pl.ds(f, 1)]

    def ag_pass(level):
        for h in HALVES:
            for s in range(2):
                for way in WAYS:
                    ag_copy[way, level - 1, h, s].wait_recv()
                    if level < 3 or s == way:
                        ag_send(way, level + 1, h, s)
            for way in WAYS:
                sb_send(way, level, h)

    def y_add(zs, h, first=False):
        p = split(jnp.swapaxes(pfull[h, zs], 0, 1))
        y = dot3(p, (chi[zs], clo[zs]))
        yp[h] = y if first else yp[h] + y

    def y_level(level, h):
        for way in WAYS:
            if (way, level, h) in sb_copy:
                sb_copy[way, level, h].wait_recv()
        for way in range(2 if 0 < level < 4 else 1):
            y_add(source(way, level), h, level == 0)

    def y_scatter(h):
        to_all(lambda peer: yp.at[h, pl.ds(pl.multiple_of(peer * 8, 8), 8)], yr.at[h], y_s.at[h], y_r.at[h], "fsdp")
        yr[h, pl.ds(f, 1)] = yp[h, pl.ds(pl.multiple_of(f * 8, 8), 8)].reshape(1, 8, COLS)

    def y_gather(h):
        span_wait(yr.at[h], y_r.at[h])
        y8[h] = total(yr.at[h])
        to_all(lambda peer: y8.at[h], yf.at[h], y_s.at[2 + h], y_r.at[2 + h], "fsdp")
        yf[h, pl.ds(f, 1)] = y8[pl.ds(h, 1)]

    ag_pass(1)
    for h in HALVES:
        y_level(0, h)
    ag_pass(2)
    span_wait(g1, g_r.at[0])
    g16[0] = total(g1)
    to_all(lambda peer: g16.at[0], g2, g_s.at[1], g_r.at[1], "z")
    g2[pl.ds(z, 1)] = g16[pl.ds(0, 1)]
    for h in HALVES:
        y_level(1, h)
    ag_pass(3)
    span_wait(g2, g_r.at[1])
    g16[1] = total(g2)
    g_copy = go(remote(g16.at[1], gs, g_s.at[3], g_r.at[3], sibling))
    for h in HALVES:
        y_level(2, h)
    g_copy.wait_recv()
    g16[2] = g16[1] + gs[...]
    to_all(lambda peer: g16.at[2], gf, g_s.at[2], g_r.at[2], "fsdp")
    gf[pl.ds(f, 1)] = g16[pl.ds(2, 1)]
    for h in HALVES:
        for way in WAYS:
            ag_copy[way, 3, h, way].wait_recv()
            sb_send(way, 4, h)
        y_level(3, h)
    for h in HALVES:
        y_level(4, h)
        y_scatter(h)
    span_wait(gf, g_r.at[2])
    M[...] = gf[...].reshape(R, R)
    for k in range(R // NB):
        if k == 4:
            y_gather(0)
            y_gather(1)
        chol_step(M, k)
    row = lax.broadcasted_iota(jnp.int32, (R, R), 0)
    col = lax.broadcasted_iota(jnp.int32, (R, R), 1)
    M[...] = jnp.where(col <= row, M[...], 0.0)
    for h in HALVES:
        span_wait(yf.at[h], y_r.at[2 + h])
    wt = dot3(split(M[...]), split(yf[...].reshape(R, COLS)))
    wt_out[...] = wt
    cs[...] = dot(jnp.ones((8, COLS), F32), wt * wt, ((1,), (1,)), HIGHEST)
    to_all(lambda peer: cs, csr, n_s, n_r, "rep")
    csr[pl.ds(r, 1)] = cs[...].reshape(1, 8, R)

    @pl.loop(0, NZ)
    def _(o):
        zs = (z + o) % NZ
        t = jnp.concatenate([pfull[0, zs], pfull[1, zs]], axis=1)
        u = dot3(split(t), split(M[...]), ((1,), (1,)))
        u_out[zs] = u
        nm_out[zs] = momb[o] - keep_share * dot(u.astype(BF16), wt_out[...].astype(BF16))

    span_wait(csr, n_r)
    inv_out[...] = 1.0 / jnp.sqrt(total(csr) / D + norm_eps)
    for copy in sends:
        copy.wait_send()
    for k, ref in enumerate((g1, g2, gf)):
        span_wait(ref, g_s.at[k])
    for h in HALVES:
        span_wait(yr.at[h], y_s.at[h])
        span_wait(yf.at[h], y_s.at[2 + h])
    span_wait(csr, n_s)


def gather(mom, grad, q):
    dma = pltpu.SemaphoreType.DMA
    vm = pltpu.VMEM
    scratch = [
        vm((NZ, PAIR, COLS), F32), vm((NZ, PAIR, COLS), BF16), vm((COLS, R), F32),
        vm((NZ, PAIR, COLS), BF16), vm((NZ, PAIR, COLS), BF16),
        vm((NZ, PAIR, R), F32), vm((NZ, OWN, R), F32), vm((2, 4, 2, 2, SUB, 128), F32), vm((2, NZ, PAIR, 128), F32),
        vm((16, 16, R), F32), vm((16, 16, R), F32), vm((NZ, 16, R), F32), vm((16, R), F32), vm((16, 16, R), F32),
        vm((R, R), F32),
        vm((2, 128, COLS), F32), vm((2, 16, 8, COLS), F32), vm((2, 16, 8, COLS), F32), vm((2, 8, COLS), F32),
        vm((3, 16, R), F32), vm((8, R), F32), vm((16, 8, R), F32),
        dma((2, NZ)), dma, dma((NZ,)), dma((NZ,)), dma((2, 4, 2, 2)), dma((2, 4, 2, 2)),
        dma((2, 4, 2, 2)), dma((2, 4, 2, 2)), dma((2, 5, 2)), dma((2, 5, 2)),
        dma((4,)), dma((4,)), dma((4,)), dma((4,)), dma, dma,
    ]
    whole, hbm = pl.BlockSpec(memory_space=pltpu.VMEM), pl.BlockSpec(memory_space=pl.ANY)
    return pl.pallas_call(
        gather_kernel,
        name="gather",
        out_shape=(
            pltpu.VMEM((NZ, PAIR, COLS), F32),
            pltpu.VMEM((NZ, PAIR, R), F32),
            pltpu.VMEM((R, COLS), F32),
            pltpu.VMEM((8, R), F32),
        ),
        in_specs=[hbm, hbm, hbm],
        out_specs=(whole, whole, whole, whole),
        scratch_shapes=scratch,
        compiler_params=pltpu.CompilerParams(
            collective_id=0, has_side_effects=True, vmem_limit_bytes=40 << 20
        ),
    )(*(pltpu.with_memory_space_constraint(x, pltpu.HBM) for x in (mom, grad, q)))


def result_kernel(
    nm, u_ref, wt_ref, inv_ref, new_mom, new_factor, update, ub, fb, wh, wl, m_sem, u_sem, f_sem
):
    def tile(i):
        return pl.ds(i * TILE, TILE)

    copies = []
    for i in range(ROWS // TILE):
        copies.append(pltpu.make_async_copy(nm.at[tile(i)], new_mom.at[tile(i)], m_sem.at[i]))
        copies[-1].start()
    inv = inv_ref[0:1, :]
    wh[...], wl[...] = split(wt_ref[...])
    for i in range(ROWS // TILE):
        scaled = split(u_ref[tile(i), :] * (inv * (-step_size * math.sqrt(FF / R))))
        ub[tile(i), :] = dot3(scaled, (wh[...], wl[...])).astype(BF16)
        copies.append(pltpu.make_async_copy(ub.at[tile(i)], update.at[tile(i)], u_sem.at[i]))
        copies[-1].start()
        if i == 0:
            fb[...] = jnp.swapaxes(wt_ref[...], 0, 1) * inv
            copies.append(pltpu.make_async_copy(fb, new_factor, f_sem))
            copies[-1].start()
    for copy in copies:
        copy.wait()


def results(nm, u, wt, inv):
    vmem, hbm = pl.BlockSpec(memory_space=pltpu.VMEM), pl.BlockSpec(memory_space=pl.ANY)
    dma = pltpu.SemaphoreType.DMA
    return pl.pallas_call(
        result_kernel,
        name="results",
        out_shape=(
            jax.ShapeDtypeStruct((ROWS, COLS), F32),
            jax.ShapeDtypeStruct((COLS, R), F32),
            jax.ShapeDtypeStruct((ROWS, COLS), BF16),
        ),
        in_specs=[vmem, vmem, vmem, vmem],
        out_specs=(hbm, hbm, hbm),
        scratch_shapes=[
            pltpu.VMEM((ROWS, COLS), BF16),
            pltpu.VMEM((COLS, R), F32),
            pltpu.VMEM((R, COLS), BF16),
            pltpu.VMEM((R, COLS), BF16),
            dma((ROWS // TILE,)),
            dma((ROWS // TILE,)),
            dma,
        ],
        compiler_params=pltpu.CompilerParams(vmem_limit_bytes=32 << 20),
    )(nm, u, wt, inv)


def local(momentum, gradient, right_factor):
    nm, u, wt, inv = gather(momentum, gradient, right_factor)
    return results(nm.reshape(ROWS, COLS), u.reshape(ROWS, R), wt, inv)


def solution(mesh):
    in_specs = (P("fsdp", "rep"), P("fsdp", "rep"), P("rep", None))
    out_specs = (P("fsdp", "rep"), P("rep", None), P("fsdp", "rep"))
    return jax.shard_map(local, mesh=mesh, in_specs=in_specs, out_specs=out_specs, check_vma=False)
```

```python
import functools
import math

import jax
import jax.numpy as jnp
from jax import lax
from jax.experimental import pallas as pl
from jax.experimental.pallas import tpu as pltpu
from jax.sharding import PartitionSpec as P

D = 8192
FF = 28672
R = 256

keep_share = 0.05
step_size = 0.5
norm_eps = 1e-06

F32 = jnp.float32
BF16 = jnp.bfloat16
MESH = pl.DeviceIdType.MESH
HIGHEST = lax.Precision.HIGHEST

ROWS = 1792
COLS = 512
NZ = 8
NF = 16
NR = 16
PAIR = ROWS // NZ
OWN = PAIR // 2
SUB = OWN // 2
NB = 32
TILE = 128


def split(x):
    hi = x.astype(BF16)
    return hi, (x - hi.astype(F32)).astype(BF16)


def dot(a, b, dims=((1,), (0,)), precision=None):
    return lax.dot_general(a, b, (dims, ((), ())), precision=precision, preferred_element_type=F32)


def dot3(a, b, dims=((1,), (0,))):
    return dot(a[0], b[0], dims) + (dot(a[1], b[0], dims) + dot(a[0], b[1], dims))


def factor_panel(rows, base):
    lane = lax.broadcasted_iota(jnp.int32, (8, 128), 1)
    sub = lax.broadcasted_iota(jnp.int32, (8, 128), 0)
    n = len(rows)
    for j in range(n):
        l0 = base + 8 * j
        half, at = l0 // 128, l0 % 128
        cols = [
            [jnp.broadcast_to(rows[i][half][:, at + c : at + c + 1], (8, 128)) for c in range(8)]
            for i in range(j, n)
        ]
        s = [
            [jnp.broadcast_to(cols[0][c][r : r + 1, :], (8, 128)) if r >= c else None for c in range(8)]
            for r in range(8)
        ]
        inv, low, solved = [None] * 8, [[None] * 8 for _ in range(8)], []
        own = (lane >= at) & (lane < at + 8)
        v = list(rows[j])
        v[half] = jnp.where(own, jnp.where(lane - at == sub, 1.0, 0.0), v[half])
        for p in range(8):
            inv[p] = lax.rsqrt(s[p][p])
            for r in range(p + 1, 8):
                low[r][p] = s[r][p] * inv[p]
            for r in range(p + 1, 8):
                for c in range(p + 1, r + 1):
                    s[r][c] = s[r][c] - low[r][p] * low[c][p]
            x = [jnp.broadcast_to(v[h][p : p + 1, :], (8, 128)) for h in range(2)]
            for q in range(p):
                x = [x[h] - low[p][q] * solved[q][h] for h in range(2)]
            solved.append([x[h] * inv[p] for h in range(2)])
        for i in range(j + 1, n):
            w, coef = list(rows[i]), []
            w[half] = jnp.where(own, 0.0, w[half])
            for p in range(8):
                t = cols[i - j][p]
                for q in range(p):
                    t = t - coef[q] * low[p][q]
                coef.append(t * inv[p])
            for p in range(8):
                w = [w[h] - coef[p] * solved[p][h] for h in range(2)]
            rows[i] = w
        out = []
        for h in range(2):
            a = solved[0][h]
            for p in range(1, 8):
                a = jnp.where(sub == p, solved[p][h], a)
            out.append(a)
        rows[j] = out
    return rows


def chol_step(M, k):
    r0, end = NB * k, NB * (k + 1)
    rows = [
        [M[r0 + 8 * j : r0 + 8 * j + 8, 128 * h : 128 * h + 128] for h in range(2)] for j in range(NB // 8)
    ]
    rows = factor_panel(rows, r0)
    for j in range(NB // 8):
        for h in range(2):
            M[r0 + 8 * j : r0 + 8 * j + 8, 128 * h : 128 * h + 128] = rows[j][h]
    if end == R:
        return
    panel = M[r0:end, :]
    row = lax.broadcasted_iota(jnp.int32, (NB, R), 0) + r0
    col = lax.broadcasted_iota(jnp.int32, (NB, R), 1)
    right = jnp.where((col < end) & (col > row), 0.0, panel)
    lo = (end // 128) * 128
    left = jnp.swapaxes(panel[:, lo:], 0, 1)[end - lo :, :]
    old = M[end:, :]
    at = lax.broadcasted_iota(jnp.int32, old.shape, 1)
    old = jnp.where((at >= r0) & (at < end), 0.0, old)
    M[end : end + NB, :] = old[:NB] - dot(left[:NB], right, precision=HIGHEST)
    if end + NB < R:
        M[end + NB :, :] = old[NB:] - dot(left[NB:], right, precision=HIGHEST)


def gather_kernel(
    mom, grad, q_hbm, nm_out, uh_out, ul_out, wt_out, inv_out,
    momb, gradb, qb, chi, clo, part, sib, rsr, pfull, gp, g1, g2, gs, gf, gh, M, yp, yr, yf, y8, g16, cs, csr, lth, ltl, wh,
    ld_sem, q_sem, sib_s, sib_r, rs_s, rs_r, ag_s, ag_r, sb_s, sb_r, g_s, g_r, y_s, y_r, n_s, n_r,
):
    f, r = lax.axis_index("fsdp"), lax.axis_index("rep")
    z, c = r // 2, r % 2
    sibling = (f, z * 2 + 1 - c)
    ring = ((f, ((z + 1) % NZ) * 2 + c), (f, ((z + NZ - 1) % NZ) * 2 + c))
    mine = pl.multiple_of(c * OWN, 8)
    other = pl.multiple_of((1 - c) * OWN, 8)
    HALVES, WAYS = range(2), range(2)
    x, y = f // 4, f % 4
    steps = sorted(((dx, dy) for dx in range(4) for dy in range(4)), key=lambda d: -(d[0] % 3 + d[0] // 3 + d[1] % 3 + d[1] // 3))
    peers = {
        "fsdp": [((x + dx) % 4) * 4 + (y + dy) % 4 for dx, dy in steps if (dx, dy) != (0, 0)],
        "z": [(z + dz) % NZ for dz in (4, 3, 5, 2, 6, 1, 7)],
    }
    peers["rep"] = [zp * 2 + cp for zp in peers["z"] for cp in (1 - c, c)] + [z * 2 + 1 - c]

    def lanes(h):
        return pl.ds(128 * h, 128)

    def sub_at(s):
        return pl.ds(pl.multiple_of(c * OWN + s * SUB, 8), SUB)

    def slot(o):
        return (o + 3) % NZ

    def remote(src, dst, ss, rs, to):
        return pltpu.make_async_remote_copy(src, dst, ss, rs, device_id=to, device_id_type=MESH)

    q_load = pltpu.make_async_copy(q_hbm, qb, q_sem)
    q_load.start()
    loads = {}
    for o in (4, 3, 5, 2, 6, 1, 7, 0):
        zd = (z + o) % NZ
        at = pl.ds(pl.multiple_of(zd * PAIR, PAIR), PAIR)
        loads[o] = (
            pltpu.make_async_copy(mom.at[at], momb.at[slot(o)], ld_sem.at[0, o]),
            pltpu.make_async_copy(grad.at[at], gradb.at[slot(o)], ld_sem.at[1, o]),
        )
        for copy in loads[o]:
            copy.start()

    barrier = pltpu.get_barrier_semaphore()

    @pl.loop(1, 16)
    def _(k):
        pl.semaphore_signal(barrier, 1, device_id=(f, (r + k) % NR), device_id_type=MESH)
        pl.semaphore_signal(barrier, 1, device_id=((f + k) % NF, r), device_id_type=MESH)

    q_load.wait()
    q = split(qb[...])
    sends = []

    def go(copy):
        copy.start()
        sends.append(copy)
        return copy

    sib_copy = {}

    def compute(o):
        for copy in loads[o]:
            copy.wait()
        combined = momb[slot(o)] + gradb[slot(o)].astype(F32)
        momb[slot(o)] = combined
        both = split(combined)
        chi[slot(o)] = both[0]
        clo[slot(o)] = both[1]
        part[o] = dot3(both, q)

    def to_sibling(o):
        sib_copy[o] = go(
            remote(part.at[o, pl.ds(other, OWN)], sib.at[o], sib_s.at[o], sib_r.at[o], sibling)
        )

    def add_sibling(o):
        sib_copy[o].wait_recv()
        part[o, pl.ds(mine, OWN)] = part[o, pl.ds(mine, OWN)] + sib[o]

    def offset(way, level):
        return level if way == 0 else (NZ - level) % NZ

    rs_copy = {}

    def rs_send(way, level, s, h):
        at = (way, level - 1, h, s)
        rs_copy[at] = go(
            remote(
                part.at[offset(way, level), sub_at(s), lanes(h)],
                rsr.at[at], rs_s.at[at], rs_r.at[at], ring[way],
            )
        )

    def rs_add(way, level, s, h):
        at = (way, level, h, s)
        rs_copy[at].wait_recv()
        o = offset(way, level)
        part[o, sub_at(s), lanes(h)] = part[o, sub_at(s), lanes(h)] + rsr[at]

    def rs_pass(level, late):
        for h in HALVES:
            for way in WAYS:
                s = way if late else 1 - way
                rs_add(way, level, s, h)
                rs_send(way, level, s, h)

    compute(4)
    compute(3)
    pl.semaphore_wait(barrier, 30)
    to_sibling(4)
    to_sibling(3)
    compute(5)
    to_sibling(5)
    add_sibling(4)
    for h in HALVES:
        for way in WAYS:
            rs_send(way, 4, way, h)
    add_sibling(3)
    for h in HALVES:
        rs_send(0, 3, 1, h)
    add_sibling(5)
    for h in HALVES:
        rs_send(1, 3, 0, h)
    compute(2)
    to_sibling(2)
    compute(6)
    to_sibling(6)
    compute(1)
    to_sibling(1)
    add_sibling(2)
    add_sibling(6)
    rs_pass(3, True)
    compute(7)
    to_sibling(7)
    rs_pass(2, False)
    compute(0)
    to_sibling(0)
    add_sibling(1)
    add_sibling(7)
    rs_pass(2, True)
    rs_pass(1, False)
    add_sibling(0)
    rs_pass(1, True)

    ag_copy, sb_copy = {}, {}

    def source(way, level):
        return slot(-level if way == 0 else level)

    def ag_send(way, level, h, s):
        at = (way, level - 1, h, s)
        ref = pfull.at[h, source(way, level - 1), sub_at(s)]
        dst = pfull.at[h, source(way, level), sub_at(s)]
        ag_copy[at] = go(remote(ref, dst, ag_s.at[at], ag_r.at[at], ring[way]))

    def sb_send(i, first, end, h=None):
        ref = pfull.at[slice(None) if h is None else pl.ds(h, 1), pl.ds(first, end - first), pl.ds(mine, OWN)]
        sb_copy[i] = go(remote(ref, ref, sb_s.at[i], sb_r.at[i], sibling))

    for h in HALVES:
        for late in (False, True):
            for way in WAYS:
                rs_add(way, 0, way if late else 1 - way, h)
        pfull[h, slot(0), pl.ds(mine, OWN), :] = part[0, pl.ds(mine, OWN), lanes(h)]
        for s in range(2):
            for way in WAYS:
                ag_send(way, 1, h, s)

    def to_all(src_of, dst, send, recv, along):
        me = {"rep": r, "fsdp": f, "z": z}[along]
        for peer in peers[along]:
            to = {"rep": (f, peer), "fsdp": (peer, r), "z": (f, peer * 2 + c)}[along]
            remote(src_of(peer), dst.at[me], send, recv, to).start()

    def span_wait(dst, sem):
        span = dst.at[pl.ds(0, dst.shape[0] - 1)]
        pltpu.make_async_copy(span, span, sem).wait()

    def total(ref):
        t = ref[0]
        for k in range(1, ref.shape[0]):
            t = t + ref[k]
        return t

    own_rows = part[0, pl.ds(mine, OWN), :]
    gp[...] = dot(own_rows, own_rows, ((0,), (0,)), HIGHEST).reshape(16, 16, R)
    to_all(lambda peer: gp.at[peer], g1, g_s.at[0], g_r.at[0], "fsdp")
    g1[pl.ds(f, 1)] = gp[pl.ds(f, 1)]

    def ag_pass(level, h):
        for s in range(2):
            for way in WAYS:
                ag_copy[way, level - 1, h, s].wait_recv()
                if level < 3 or s == way:
                    ag_send(way, level + 1, h, s)

    def y_add(first, end, h):
        deep = (end - first) * PAIR
        p = split(jnp.swapaxes(pfull[h, first:end].reshape(deep, 128), 0, 1))
        return dot3(p, (chi[first:end].reshape(deep, COLS), clo[first:end].reshape(deep, COLS)))

    def y_scatter(h):
        to_all(lambda peer: yp.at[h, pl.ds(pl.multiple_of(peer * 8, 8), 8)], yr.at[h], y_s.at[h], y_r.at[h], "fsdp")
        yr[h, pl.ds(f, 1)] = yp[h, pl.ds(pl.multiple_of(f * 8, 8), 8)].reshape(1, 8, COLS)

    def y_gather(h):
        span_wait(yr.at[h], y_r.at[h])
        y8[h] = total(yr.at[h])
        to_all(lambda peer: y8.at[h], yf.at[h], y_s.at[2 + h], y_r.at[2 + h], "fsdp")
        yf[h, pl.ds(f, 1)] = y8[pl.ds(h, 1)]

    ag_pass(1, 0)
    ag_pass(1, 1)
    ag_pass(2, 0)
    span_wait(g1, g_r.at[0])
    g16[...] = total(g1)
    my_half = pl.ds(pl.multiple_of(c * 8, 8), 8)
    g_copy = go(
        remote(g16.at[pl.ds(pl.multiple_of((1 - c) * 8, 8), 8)], gs, g_s.at[3], g_r.at[3], sibling)
    )
    ag_pass(2, 1)
    sb_send(0, 1, 6)
    g_copy.wait_recv()
    gh[0] = g16[my_half, :] + gs[...]
    to_all(lambda peer: gh.at[0], g2, g_s.at[1], g_r.at[1], "z")
    g2[pl.ds(z, 1)] = gh[pl.ds(0, 1)]
    ag_pass(3, 0)
    ag_pass(3, 1)
    sb_send(1, 0, 1)
    sb_send(2, 6, 7)
    sb_copy[0].wait_recv()
    for h in HALVES:
        yp[h] = y_add(1, 6, h)
    for h in HALVES:
        for way in WAYS:
            ag_copy[way, 3, h, way].wait_recv()
        sb_send(3 + h, 7, 8, h)
    span_wait(g2, g_r.at[1])
    gh[1] = total(g2)
    to_all(lambda peer: gh.at[1], gf.at[c], g_s.at[2], g_r.at[2], "fsdp")
    gf[c, pl.ds(f, 1)] = gh[pl.ds(1, 1)]
    sb_copy[1].wait_recv()
    sb_copy[2].wait_recv()
    for h in HALVES:
        yp[h] = yp[h] + (y_add(0, 1, h) + y_add(6, 7, h))
    for h in HALVES:
        sb_copy[3 + h].wait_recv()
        yp[h] = yp[h] + y_add(7, 8, h)
        y_scatter(h)
    span_wait(gf.at[0], g_r.at[2])
    g_copy = go(remote(gf.at[c], gf.at[c], g_s.at[4], g_r.at[4], sibling))
    for h in HALVES:
        y_gather(h)
    g_copy.wait_recv()
    M[...] = jnp.stack([gf[0], gf[1]], axis=1).reshape(R, R)
    for k in range(R // NB):
        chol_step(M, k)
    row = lax.broadcasted_iota(jnp.int32, (R, R), 0)
    col = lax.broadcasted_iota(jnp.int32, (R, R), 1)
    M[...] = jnp.where(col <= row, M[...], 0.0)
    for h in HALVES:
        span_wait(yf.at[h], y_r.at[2 + h])
    wt = dot3(split(M[...]), split(yf[...].reshape(R, COLS)))
    wt_out[...] = wt
    square = wt * wt
    square = (square[:, :128] + square[:, 128:256]) + (square[:, 256:384] + square[:, 384:])
    cs[...] = jnp.broadcast_to(jnp.sum(jnp.swapaxes(square, 0, 1), axis=0, keepdims=True), (8, R))
    to_all(lambda peer: cs, csr, n_s, n_r, "rep")
    csr[pl.ds(r, 1)] = cs[...].reshape(1, 8, R)

    lth[...], ltl[...] = split(jnp.swapaxes(M[...], 0, 1))
    wh[...] = wt.astype(BF16)

    @pl.loop(0, NZ)
    def _(k):
        zs = (z + k + NZ - 3) % NZ
        t = jnp.concatenate([pfull[0, k], pfull[1, k]], axis=1)
        u = dot3(split(t), (lth[...], ltl[...]))
        u = split(u)
        uh_out[zs] = u[0]
        ul_out[zs] = u[1]
        nm_out[zs] = momb[k] - keep_share * dot(u[0], wh[...])

    span_wait(csr, n_r)
    inv_out[...] = 1.0 / jnp.sqrt(total(csr) / D + norm_eps)
    for copy in sends:
        copy.wait_send()
    for k, ref in enumerate((g1, g2, gf.at[0])):
        span_wait(ref, g_s.at[k])
    for h in HALVES:
        span_wait(yr.at[h], y_s.at[h])
        span_wait(yf.at[h], y_s.at[2 + h])
    span_wait(csr, n_s)


def gather(mom, grad, q):
    dma = pltpu.SemaphoreType.DMA
    vm = pltpu.VMEM
    scratch = [
        vm((NZ, PAIR, COLS), F32), vm((NZ, PAIR, COLS), BF16), vm((COLS, R), F32),
        vm((NZ, PAIR, COLS), BF16), vm((NZ, PAIR, COLS), BF16),
        vm((NZ, PAIR, R), F32), vm((NZ, OWN, R), F32), vm((2, 4, 2, 2, SUB, 128), F32), vm((2, NZ, PAIR, 128), F32),
        vm((16, 16, R), F32), vm((16, 16, R), F32), vm((NZ, 8, R), F32), vm((8, R), F32), vm((2, 16, 8, R), F32),
        vm((2, 8, R), F32),
        vm((R, R), F32),
        vm((2, 128, COLS), F32), vm((2, 16, 8, COLS), F32), vm((2, 16, 8, COLS), F32), vm((2, 8, COLS), F32),
        vm((16, R), F32), vm((8, R), F32), vm((16, 8, R), F32),
        vm((R, R), BF16), vm((R, R), BF16), vm((R, COLS), BF16),
        dma((2, NZ)), dma, dma((NZ,)), dma((NZ,)), dma((2, 4, 2, 2)), dma((2, 4, 2, 2)),
        dma((2, 4, 2, 2)), dma((2, 4, 2, 2)), dma((5,)), dma((5,)),
        dma((5,)), dma((5,)), dma((4,)), dma((4,)), dma, dma,
    ]
    whole, hbm = pl.BlockSpec(memory_space=pltpu.VMEM), pl.BlockSpec(memory_space=pl.ANY)
    return pl.pallas_call(
        gather_kernel,
        name="gather",
        out_shape=(
            pltpu.VMEM((NZ, PAIR, COLS), F32),
            pltpu.VMEM((NZ, PAIR, R), BF16),
            pltpu.VMEM((NZ, PAIR, R), BF16),
            pltpu.VMEM((R, COLS), F32),
            pltpu.VMEM((8, R), F32),
        ),
        in_specs=[hbm, hbm, hbm],
        out_specs=(whole,) * 5,
        scratch_shapes=scratch,
        compiler_params=pltpu.CompilerParams(
            collective_id=0, has_side_effects=True, vmem_limit_bytes=40 << 20
        ),
    )(*(pltpu.with_memory_space_constraint(x, pltpu.HBM) for x in (mom, grad, q)))


def result_kernel(
    nm, uh, ul, wt_ref, inv_ref, new_mom, new_factor, update, ub, fb, wh, wl, m_sem, u_sem, f_sem
):
    steps = ROWS // TILE

    def tile(i):
        return pl.ds(i * TILE, TILE)

    copies = []

    def go(src, dst, sem):
        copies.append(pltpu.make_async_copy(src, dst, sem))
        copies[-1].start()

    for i in range(0, steps, 2):
        go(nm.at[tile(i)], new_mom.at[tile(i)], m_sem.at[i])
    inv = jnp.swapaxes(inv_ref[...], 0, 1)[:, 0:1]
    factor = wt_ref[...] * inv
    wh[...], wl[...] = split(factor * (-step_size * math.sqrt(FF / R)))
    for i in range(steps):
        ub[tile(i), :] = dot3((uh[tile(i), :], ul[tile(i), :]), (wh[...], wl[...])).astype(BF16)
        go(ub.at[tile(i)], update.at[tile(i)], u_sem.at[i])
        if i < steps // 2:
            go(nm.at[tile(2 * i + 1)], new_mom.at[tile(2 * i + 1)], m_sem.at[2 * i + 1])
        if i == 0:
            fb[...] = jnp.swapaxes(wt_ref[...] * inv, 0, 1)
            go(fb, new_factor, f_sem)
    for copy in copies:
        copy.wait()


def results(nm, uh, ul, wt, inv):
    vmem, hbm = pl.BlockSpec(memory_space=pltpu.VMEM), pl.BlockSpec(memory_space=pl.ANY)
    dma = pltpu.SemaphoreType.DMA
    return pl.pallas_call(
        result_kernel,
        name="results",
        out_shape=(
            jax.ShapeDtypeStruct((ROWS, COLS), F32),
            jax.ShapeDtypeStruct((COLS, R), F32),
            jax.ShapeDtypeStruct((ROWS, COLS), BF16),
        ),
        in_specs=[vmem] * 5,
        out_specs=(hbm, hbm, hbm),
        scratch_shapes=[
            pltpu.VMEM((ROWS, COLS), BF16),
            pltpu.VMEM((COLS, R), F32),
            pltpu.VMEM((R, COLS), BF16),
            pltpu.VMEM((R, COLS), BF16),
            dma((ROWS // TILE,)),
            dma((ROWS // TILE,)),
            dma,
        ],
        compiler_params=pltpu.CompilerParams(vmem_limit_bytes=32 << 20),
    )(nm, uh, ul, wt, inv)


def local(momentum, gradient, right_factor):
    nm, uh, ul, wt, inv = gather(momentum, gradient, right_factor)
    return results(nm.reshape(ROWS, COLS), uh.reshape(ROWS, R), ul.reshape(ROWS, R), wt, inv)


def solution(mesh):
    in_specs = (P("fsdp", "rep"), P("fsdp", "rep"), P("rep", None))
    out_specs = (P("fsdp", "rep"), P("rep", None), P("fsdp", "rep"))
    return jax.shard_map(local, mesh=mesh, in_specs=in_specs, out_specs=out_specs, check_vma=False)
```

```python
import functools
import math

import jax
import jax.numpy as jnp
from jax import lax
from jax.experimental import pallas as pl
from jax.experimental.pallas import tpu as pltpu
from jax.sharding import PartitionSpec as P

D = 8192
FF = 28672
R = 256

keep_share = 0.05
step_size = 0.5
norm_eps = 1e-06

F32 = jnp.float32
BF16 = jnp.bfloat16
MESH = pl.DeviceIdType.MESH
HIGHEST = lax.Precision.HIGHEST

ROWS = 1792
COLS = 512
NZ = 8
NF = 16
NR = 16
PAIR = ROWS // NZ
OWN = PAIR // 2
SUB = OWN // 2
NB = 32
TILE = 128


def split(x):
    hi = x.astype(BF16)
    return hi, (x - hi.astype(F32)).astype(BF16)


def dot(a, b, dims=((1,), (0,)), precision=None):
    return lax.dot_general(a, b, (dims, ((), ())), precision=precision, preferred_element_type=F32)


def dot3(a, b, dims=((1,), (0,))):
    return dot(a[0], b[0], dims) + (dot(a[1], b[0], dims) + dot(a[0], b[1], dims))


def factor_panel(rows, base):
    lane = lax.broadcasted_iota(jnp.int32, (8, 128), 1)
    sub = lax.broadcasted_iota(jnp.int32, (8, 128), 0)
    n = len(rows)
    for j in range(n):
        l0 = base + 8 * j
        half, at = l0 // 128, l0 % 128
        cols = [
            [jnp.broadcast_to(rows[i][half][:, at + c : at + c + 1], (8, 128)) for c in range(8)]
            for i in range(j, n)
        ]
        s = [
            [jnp.broadcast_to(cols[0][c][r : r + 1, :], (8, 128)) if r >= c else None for c in range(8)]
            for r in range(8)
        ]
        inv, low, solved = [None] * 8, [[None] * 8 for _ in range(8)], []
        own = (lane >= at) & (lane < at + 8)
        v = list(rows[j])
        v[half] = jnp.where(own, jnp.where(lane - at == sub, 1.0, 0.0), v[half])
        for p in range(8):
            inv[p] = lax.rsqrt(s[p][p])
            for r in range(p + 1, 8):
                low[r][p] = s[r][p] * inv[p]
            for r in range(p + 1, 8):
                for c in range(p + 1, r + 1):
                    s[r][c] = s[r][c] - low[r][p] * low[c][p]
            x = [jnp.broadcast_to(v[h][p : p + 1, :], (8, 128)) for h in range(2)]
            for q in range(p):
                x = [x[h] - low[p][q] * solved[q][h] for h in range(2)]
            solved.append([x[h] * inv[p] for h in range(2)])
        for i in range(j + 1, n):
            w, coef = list(rows[i]), []
            w[half] = jnp.where(own, 0.0, w[half])
            for p in range(8):
                t = cols[i - j][p]
                for q in range(p):
                    t = t - coef[q] * low[p][q]
                coef.append(t * inv[p])
            for p in range(8):
                w = [w[h] - coef[p] * solved[p][h] for h in range(2)]
            rows[i] = w
        out = []
        for h in range(2):
            a = solved[0][h]
            for p in range(1, 8):
                a = jnp.where(sub == p, solved[p][h], a)
            out.append(a)
        rows[j] = out
    return rows


def chol_step(M, k):
    r0, end = NB * k, NB * (k + 1)
    rows = [
        [M[r0 + 8 * j : r0 + 8 * j + 8, 128 * h : 128 * h + 128] for h in range(2)] for j in range(NB // 8)
    ]
    rows = factor_panel(rows, r0)
    for j in range(NB // 8):
        for h in range(2):
            M[r0 + 8 * j : r0 + 8 * j + 8, 128 * h : 128 * h + 128] = rows[j][h]
    if end == R:
        return
    panel = M[r0:end, :]
    row = lax.broadcasted_iota(jnp.int32, (NB, R), 0) + r0
    col = lax.broadcasted_iota(jnp.int32, (NB, R), 1)
    right = jnp.where((col < end) & (col > row), 0.0, panel)
    lo = (end // 128) * 128
    left = jnp.swapaxes(panel[:, lo:], 0, 1)[end - lo :, :]
    old = M[end:, :]
    at = lax.broadcasted_iota(jnp.int32, old.shape, 1)
    old = jnp.where((at >= r0) & (at < end), 0.0, old)
    M[end : end + NB, :] = old[:NB] - dot(left[:NB], right, precision=HIGHEST)
    if end + NB < R:
        M[end + NB :, :] = old[NB:] - dot(left[NB:], right, precision=HIGHEST)


def gather_kernel(
    mom, grad, q_hbm, nm_out, uh_out, ul_out, wt_out, inv_out,
    momb, gradb, qb, chi, clo, part, sib, rsr, pfull, gp, g1, g2, gs, gf, gh, M, yp, yr, yf, y8, g16, cs, csr, lth, ltl, wh,
    ld_sem, q_sem, sib_s, sib_r, rs_s, rs_r, ag_s, ag_r, sb_s, sb_r, g_s, g_r, y_s, y_r, n_s, n_r,
):
    f, r = lax.axis_index("fsdp"), lax.axis_index("rep")
    z, c = r // 2, r % 2
    sibling = (f, z * 2 + 1 - c)
    ring = ((f, ((z + 1) % NZ) * 2 + c), (f, ((z + NZ - 1) % NZ) * 2 + c))
    mine = pl.multiple_of(c * OWN, 8)
    other = pl.multiple_of((1 - c) * OWN, 8)
    HALVES, WAYS = range(2), range(2)
    x, y = f // 4, f % 4
    steps = sorted(((dx, dy) for dx in range(4) for dy in range(4)), key=lambda d: -(d[0] % 3 + d[0] // 3 + d[1] % 3 + d[1] // 3))
    peers = {
        "fsdp": [((x + dx) % 4) * 4 + (y + dy) % 4 for dx, dy in steps if (dx, dy) != (0, 0)],
        "z": [(z + dz) % NZ for dz in (4, 3, 5, 2, 6, 1, 7)],
    }
    peers["rep"] = [zp * 2 + cp for zp in peers["z"] for cp in (1 - c, c)] + [z * 2 + 1 - c]

    def lanes(h):
        return pl.ds(128 * h, 128)

    def sub_at(s):
        return pl.ds(pl.multiple_of(c * OWN + s * SUB, 8), SUB)

    def slot(o):
        return (o + 3) % NZ

    def remote(src, dst, ss, rs, to):
        return pltpu.make_async_remote_copy(src, dst, ss, rs, device_id=to, device_id_type=MESH)

    q_load = pltpu.make_async_copy(q_hbm, qb, q_sem)
    q_load.start()
    loads = {}
    for o in (4, 3, 5, 2, 6, 1, 7, 0):
        zd = (z + o) % NZ
        at = pl.ds(pl.multiple_of(zd * PAIR, PAIR), PAIR)
        loads[o] = (
            pltpu.make_async_copy(mom.at[at], momb.at[slot(o)], ld_sem.at[0, o]),
            pltpu.make_async_copy(grad.at[at], gradb.at[slot(o)], ld_sem.at[1, o]),
        )
        for copy in loads[o]:
            copy.start()

    barrier = pltpu.get_barrier_semaphore()

    @pl.loop(1, 16)
    def _(k):
        pl.semaphore_signal(barrier, 1, device_id=(f, (r + k) % NR), device_id_type=MESH)
        pl.semaphore_signal(barrier, 1, device_id=((f + k) % NF, r), device_id_type=MESH)

    q_load.wait()
    q = split(qb[...])
    sends = []

    def go(copy):
        copy.start()
        sends.append(copy)
        return copy

    sib_copy = {}

    def compute(o):
        for copy in loads[o]:
            copy.wait()
        combined = momb[slot(o)] + gradb[slot(o)].astype(F32)
        momb[slot(o)] = combined
        both = split(combined)
        chi[slot(o)] = both[0]
        clo[slot(o)] = both[1]
        part[o] = dot3(both, q)

    def to_sibling(o):
        sib_copy[o] = go(
            remote(part.at[o, pl.ds(other, OWN)], sib.at[o], sib_s.at[o], sib_r.at[o], sibling)
        )

    def add_sibling(o):
        sib_copy[o].wait_recv()
        part[o, pl.ds(mine, OWN)] = part[o, pl.ds(mine, OWN)] + sib[o]

    def offset(way, level):
        return level if way == 0 else (NZ - level) % NZ

    rs_copy = {}

    def rs_send(way, level, s, h):
        at = (way, level - 1, h, s)
        rs_copy[at] = go(
            remote(
                part.at[offset(way, level), sub_at(s), lanes(h)],
                rsr.at[at], rs_s.at[at], rs_r.at[at], ring[way],
            )
        )

    def rs_add(way, level, s, h):
        at = (way, level, h, s)
        rs_copy[at].wait_recv()
        o = offset(way, level)
        part[o, sub_at(s), lanes(h)] = part[o, sub_at(s), lanes(h)] + rsr[at]

    def rs_pass(level, late):
        for h in HALVES:
            for way in WAYS:
                s = way if late else 1 - way
                rs_add(way, level, s, h)
                rs_send(way, level, s, h)

    compute(4)
    compute(3)
    pl.semaphore_wait(barrier, 30)
    to_sibling(4)
    to_sibling(3)
    compute(5)
    to_sibling(5)
    add_sibling(4)
    for h in HALVES:
        for way in WAYS:
            rs_send(way, 4, way, h)
    add_sibling(3)
    for h in HALVES:
        rs_send(0, 3, 1, h)
    add_sibling(5)
    for h in HALVES:
        rs_send(1, 3, 0, h)
    compute(2)
    to_sibling(2)
    compute(6)
    to_sibling(6)
    compute(1)
    to_sibling(1)
    add_sibling(2)
    add_sibling(6)
    rs_pass(3, True)
    compute(7)
    to_sibling(7)
    rs_pass(2, False)
    compute(0)
    to_sibling(0)
    add_sibling(1)
    add_sibling(7)
    rs_pass(2, True)
    rs_pass(1, False)
    add_sibling(0)
    rs_pass(1, True)

    ag_copy, sb_copy = {}, {}

    def source(way, level):
        return slot(-level if way == 0 else level)

    def ag_send(way, level, h, s):
        at = (way, level - 1, h, s)
        ref = pfull.at[h, source(way, level - 1), sub_at(s)]
        dst = pfull.at[h, source(way, level), sub_at(s)]
        ag_copy[at] = go(remote(ref, dst, ag_s.at[at], ag_r.at[at], ring[way]))

    def sb_send(i, first, end, h=None):
        ref = pfull.at[slice(None) if h is None else pl.ds(h, 1), pl.ds(first, end - first), pl.ds(mine, OWN)]
        sb_copy[i] = go(remote(ref, ref, sb_s.at[i], sb_r.at[i], sibling))

    for h in HALVES:
        for late in (False, True):
            for way in WAYS:
                rs_add(way, 0, way if late else 1 - way, h)
        pfull[h, slot(0), pl.ds(mine, OWN), :] = part[0, pl.ds(mine, OWN), lanes(h)]
        for s in range(2):
            for way in WAYS:
                ag_send(way, 1, h, s)

    def to_all(src_of, dst, send, recv, along):
        me = {"rep": r, "fsdp": f, "z": z}[along]
        for peer in peers[along]:
            to = {"rep": (f, peer), "fsdp": (peer, r), "z": (f, peer * 2 + c)}[along]
            remote(src_of(peer), dst.at[me], send, recv, to).start()

    def span_wait(dst, sem):
        span = dst.at[pl.ds(0, dst.shape[0] - 1)]
        pltpu.make_async_copy(span, span, sem).wait()

    def total(ref):
        t = ref[0]
        for k in range(1, ref.shape[0]):
            t = t + ref[k]
        return t

    own_rows = part[0, pl.ds(mine, OWN), :]
    gp[...] = dot(own_rows, own_rows, ((0,), (0,)), HIGHEST).reshape(16, 16, R)
    to_all(lambda peer: gp.at[peer], g1, g_s.at[0], g_r.at[0], "fsdp")
    g1[pl.ds(f, 1)] = gp[pl.ds(f, 1)]

    def ag_pass(level, h):
        for s in range(2):
            for way in WAYS:
                ag_copy[way, level - 1, h, s].wait_recv()
                if level < 3 or s == way:
                    ag_send(way, level + 1, h, s)

    def y_add(first, end, h):
        deep = (end - first) * PAIR
        p = split(jnp.swapaxes(pfull[h, first:end].reshape(deep, 128), 0, 1))
        return dot3(p, (chi[first:end].reshape(deep, COLS), clo[first:end].reshape(deep, COLS)))

    def y_scatter(h):
        to_all(lambda peer: yp.at[h, pl.ds(pl.multiple_of(peer * 8, 8), 8)], yr.at[h], y_s.at[h], y_r.at[h], "fsdp")
        yr[h, pl.ds(f, 1)] = yp[h, pl.ds(pl.multiple_of(f * 8, 8), 8)].reshape(1, 8, COLS)

    def y_gather(h):
        span_wait(yr.at[h], y_r.at[h])
        y8[h] = total(yr.at[h])
        to_all(lambda peer: y8.at[h], yf.at[h], y_s.at[2 + h], y_r.at[2 + h], "fsdp")
        yf[h, pl.ds(f, 1)] = y8[pl.ds(h, 1)]

    ag_pass(1, 0)
    ag_pass(1, 1)
    ag_pass(2, 0)
    span_wait(g1, g_r.at[0])
    g16[...] = total(g1)
    my_half = pl.ds(pl.multiple_of(c * 8, 8), 8)
    g_copy = go(
        remote(g16.at[pl.ds(pl.multiple_of((1 - c) * 8, 8), 8)], gs, g_s.at[3], g_r.at[3], sibling)
    )
    ag_pass(2, 1)
    sb_send(0, 1, 6)
    g_copy.wait_recv()
    gh[0] = g16[my_half, :] + gs[...]
    to_all(lambda peer: gh.at[0], g2, g_s.at[1], g_r.at[1], "z")
    g2[pl.ds(z, 1)] = gh[pl.ds(0, 1)]
    ag_pass(3, 0)
    ag_pass(3, 1)
    sb_send(1, 0, 1)
    sb_send(2, 6, 7)
    sb_copy[0].wait_recv()
    for h in HALVES:
        yp[h] = y_add(1, 6, h)
    for h in HALVES:
        for way in WAYS:
            ag_copy[way, 3, h, way].wait_recv()
        sb_send(3 + h, 7, 8, h)
    span_wait(g2, g_r.at[1])
    gh[1] = total(g2)
    to_all(lambda peer: gh.at[1], gf.at[c], g_s.at[2], g_r.at[2], "fsdp")
    gf[c, pl.ds(f, 1)] = gh[pl.ds(1, 1)]
    sb_copy[1].wait_recv()
    sb_copy[2].wait_recv()
    for h in HALVES:
        yp[h] = yp[h] + (y_add(0, 1, h) + y_add(6, 7, h))
    for h in HALVES:
        sb_copy[3 + h].wait_recv()
        yp[h] = yp[h] + y_add(7, 8, h)
        y_scatter(h)
    span_wait(gf.at[0], g_r.at[2])
    g_copy = go(remote(gf.at[c], gf.at[c], g_s.at[4], g_r.at[4], sibling))
    for h in HALVES:
        y_gather(h)
    g_copy.wait_recv()
    M[...] = jnp.stack([gf[0], gf[1]], axis=1).reshape(R, R)
    for k in range(R // NB):
        chol_step(M, k)
    row = lax.broadcasted_iota(jnp.int32, (R, R), 0)
    col = lax.broadcasted_iota(jnp.int32, (R, R), 1)
    M[...] = jnp.where(col <= row, M[...], 0.0)
    for h in HALVES:
        span_wait(yf.at[h], y_r.at[2 + h])
    wt = dot3(split(M[...]), split(yf[...].reshape(R, COLS)))
    wt_out[...] = wt
    square = wt * wt
    square = (square[:, :128] + square[:, 128:256]) + (square[:, 256:384] + square[:, 384:])
    cs[...] = jnp.sum(jnp.swapaxes(square, 0, 1), axis=0, keepdims=True)
    to_all(lambda peer: cs, csr, n_s, n_r, "rep")
    csr[pl.ds(r, 1)] = cs[...].reshape(1, 1, R)

    lth[...], ltl[...] = split(jnp.swapaxes(M[...], 0, 1))
    wh[...] = wt.astype(BF16)

    @pl.loop(0, NZ)
    def _(k):
        zs = (z + k + NZ - 3) % NZ
        t = jnp.concatenate([pfull[0, k], pfull[1, k]], axis=1)
        u = dot3(split(t), (lth[...], ltl[...]))
        u = split(u)
        uh_out[zs] = u[0]
        ul_out[zs] = u[1]
        nm_out[zs] = momb[k] - keep_share * dot(u[0], wh[...])

    span_wait(csr, n_r)
    inv_out[...] = jnp.broadcast_to(1.0 / jnp.sqrt(total(csr) / D + norm_eps), (8, R))
    for copy in sends:
        copy.wait_send()
    for k, ref in enumerate((g1, g2, gf.at[0])):
        span_wait(ref, g_s.at[k])
    for h in HALVES:
        span_wait(yr.at[h], y_s.at[h])
        span_wait(yf.at[h], y_s.at[2 + h])
    span_wait(csr, n_s)


def gather(mom, grad, q):
    dma = pltpu.SemaphoreType.DMA
    vm = pltpu.VMEM
    scratch = [
        vm((NZ, PAIR, COLS), F32), vm((NZ, PAIR, COLS), BF16), vm((COLS, R), F32),
        vm((NZ, PAIR, COLS), BF16), vm((NZ, PAIR, COLS), BF16),
        vm((NZ, PAIR, R), F32), vm((NZ, OWN, R), F32), vm((2, 4, 2, 2, SUB, 128), F32), vm((2, NZ, PAIR, 128), F32),
        vm((16, 16, R), F32), vm((16, 16, R), F32), vm((NZ, 8, R), F32), vm((8, R), F32), vm((2, 16, 8, R), F32),
        vm((2, 8, R), F32),
        vm((R, R), F32),
        vm((2, 128, COLS), F32), vm((2, 16, 8, COLS), F32), vm((2, 16, 8, COLS), F32), vm((2, 8, COLS), F32),
        vm((16, R), F32), vm((1, R), F32), vm((16, 1, R), F32),
        vm((R, R), BF16), vm((R, R), BF16), vm((R, COLS), BF16),
        dma((2, NZ)), dma, dma((NZ,)), dma((NZ,)), dma((2, 4, 2, 2)), dma((2, 4, 2, 2)),
        dma((2, 4, 2, 2)), dma((2, 4, 2, 2)), dma((5,)), dma((5,)),
        dma((5,)), dma((5,)), dma((4,)), dma((4,)), dma, dma,
    ]
    whole, hbm = pl.BlockSpec(memory_space=pltpu.VMEM), pl.BlockSpec(memory_space=pl.ANY)
    return pl.pallas_call(
        gather_kernel,
        name="gather",
        out_shape=(
            pltpu.VMEM((NZ, PAIR, COLS), F32),
            pltpu.VMEM((NZ, PAIR, R), BF16),
            pltpu.VMEM((NZ, PAIR, R), BF16),
            pltpu.VMEM((R, COLS), F32),
            pltpu.VMEM((8, R), F32),
        ),
        in_specs=[hbm, hbm, hbm],
        out_specs=(whole,) * 5,
        scratch_shapes=scratch,
        compiler_params=pltpu.CompilerParams(
            collective_id=0, has_side_effects=True, vmem_limit_bytes=40 << 20
        ),
    )(*(pltpu.with_memory_space_constraint(x, pltpu.HBM) for x in (mom, grad, q)))


def result_kernel(
    nm, uh, ul, wt_ref, inv_ref, new_mom, new_factor, update, ub, fb, wh, wl, m_sem, u_sem, f_sem
):
    steps = ROWS // TILE

    def tile(i):
        return pl.ds(i * TILE, TILE)

    copies = []

    def go(src, dst, sem):
        copies.append(pltpu.make_async_copy(src, dst, sem))
        copies[-1].start()

    for i in range(0, steps, 2):
        go(nm.at[tile(i)], new_mom.at[tile(i)], m_sem.at[i])
    inv = jnp.swapaxes(inv_ref[...], 0, 1)[:, 0:1]
    factor = wt_ref[...] * inv
    wh[...], wl[...] = split(factor * (-step_size * math.sqrt(FF / R)))
    for i in range(steps):
        ub[tile(i), :] = dot3((uh[tile(i), :], ul[tile(i), :]), (wh[...], wl[...])).astype(BF16)
        go(ub.at[tile(i)], update.at[tile(i)], u_sem.at[i])
        if i < steps // 2:
            go(nm.at[tile(2 * i + 1)], new_mom.at[tile(2 * i + 1)], m_sem.at[2 * i + 1])
        if i == 0:
            fb[...] = jnp.swapaxes(wt_ref[...] * inv, 0, 1)
            go(fb, new_factor, f_sem)
    for copy in copies:
        copy.wait()


def results(nm, uh, ul, wt, inv):
    vmem, hbm = pl.BlockSpec(memory_space=pltpu.VMEM), pl.BlockSpec(memory_space=pl.ANY)
    dma = pltpu.SemaphoreType.DMA
    return pl.pallas_call(
        result_kernel,
        name="results",
        out_shape=(
            jax.ShapeDtypeStruct((ROWS, COLS), F32),
            jax.ShapeDtypeStruct((COLS, R), F32),
            jax.ShapeDtypeStruct((ROWS, COLS), BF16),
        ),
        in_specs=[vmem] * 5,
        out_specs=(hbm, hbm, hbm),
        scratch_shapes=[
            pltpu.VMEM((ROWS, COLS), BF16),
            pltpu.VMEM((COLS, R), F32),
            pltpu.VMEM((R, COLS), BF16),
            pltpu.VMEM((R, COLS), BF16),
            dma((ROWS // TILE,)),
            dma((ROWS // TILE,)),
            dma,
        ],
        compiler_params=pltpu.CompilerParams(vmem_limit_bytes=32 << 20),
    )(nm, uh, ul, wt, inv)


def local(momentum, gradient, right_factor):
    nm, uh, ul, wt, inv = gather(momentum, gradient, right_factor)
    return results(nm.reshape(ROWS, COLS), uh.reshape(ROWS, R), ul.reshape(ROWS, R), wt, inv)


def solution(mesh):
    in_specs = (P("fsdp", "rep"), P("fsdp", "rep"), P("rep", None))
    out_specs = (P("fsdp", "rep"), P("rep", None), P("fsdp", "rep"))
    return jax.shard_map(local, mesh=mesh, in_specs=in_specs, out_specs=out_specs, check_vma=False)
```
